512 devices in a mesh: row: 16 (over x_hi, y), col: 32 (over z, x_lo, core).
Axes of the slice: x: 4 (x_hi: 2, x_lo: 2; x = x_hi * 2 + x_lo), y: 8, z: 8, core: 2. Of those that a mesh axis runs over, the one named last changes fastest.
Arguments:
- density: float32 [4096, 4096], P('row', 'col'), may hold values from -1 to 1
- pattern: int32 [32, 32], P('row', 'col'), may hold values from 0 to 1, as said below
- keep_mask: int32 [32, 32], P('row', 'col'), may hold values from 0 to 1, as said below
Outputs:
- purified: float32 [4096, 4096], P('row', 'col')
The draws below stay inside these ranges and needn't reach their ends.
Inputs may be any that keep to these rules, and one draw needn't show every extreme that they name: `pattern`: symmetric, with ones on the diagonal. `keep_mask`: symmetric, with ones on the diagonal.
All inputs are finite; a program needn't handle non-finite values.
Results may differ from the reference program's by a relative error of at most 0.00014.
Values sent between devices are 32-bit elements; how exact they have to be, the bound alone decides.
A program may use at most 64 MiB of HBM per device.

```python
import math
import jax
import jax.numpy as jnp
from jax import lax

BLOCK = 128
STEPS = 2
NB = 32
ORDER = 4096


def block_mask(key, cut):
    raw = jax.random.randint(key, (NB, NB), 0, 10)
    upper = (raw < cut).astype(jnp.int32)
    both = jnp.maximum(upper, upper.T)
    diag = (lax.broadcasted_iota(jnp.int32, (NB, NB), 0) == lax.broadcasted_iota(jnp.int32, (NB, NB), 1)).astype(jnp.int32)
    return jnp.maximum(both, diag)


def draw_pattern(key, part):
    key = jax.random.fold_in(key, 5)
    return block_mask(key, 3)


def draw_keep_mask(key, part):
    key = jax.random.fold_in(key, 7)
    return block_mask(key, 6)


def draw_density(key, part):
    key = jax.random.fold_in(key, 11)
    noise = jax.random.normal(key, (ORDER, ORDER), jnp.float32)
    scale = 0.45 / math.sqrt(2.0 * ORDER)
    diag = (lax.broadcasted_iota(jnp.int32, (ORDER, ORDER), 0) == lax.broadcasted_iota(jnp.int32, (ORDER, ORDER), 1)).astype(jnp.float32)
    return (noise + noise.T) * scale + 0.5 * diag


def setup_inputs(seed: int = 0) -> dict:
    splits = jax.random.split(jax.random.key(seed), 4)
    density = draw_density(jax.random.fold_in(splits[3], 71), 0)
    pattern = draw_pattern(jax.random.fold_in(splits[3], 71), 0)
    keep_mask = draw_keep_mask(jax.random.fold_in(splits[3], 71), 0)
    return {"density": density, "pattern": pattern, "keep_mask": keep_mask}


def widen(mask, block):
    rows, cols = mask.shape
    full = jnp.broadcast_to(mask.astype(jnp.float32)[:, None, :, None], (rows, block, cols, block))
    return full.reshape(rows * block, cols * block)


def reference(density, pattern, keep_mask):
    keep = widen(keep_mask, BLOCK)
    current = density * widen(pattern, BLOCK)
    for step in range(STEPS):
        square = keep * jnp.dot(current, current, precision=lax.Precision.HIGHEST, preferred_element_type=jnp.float32)
        cube = keep * jnp.dot(current, square, precision=lax.Precision.HIGHEST, preferred_element_type=jnp.float32)
        current = 3.0 * square - 2.0 * cube
    return current
```

```python
import functools

import jax
import jax.numpy as jnp
from jax import lax
from jax.experimental import pallas as pl
from jax.experimental.pallas import tpu as pltpu
from jax.sharding import PartitionSpec as P

STEPS = 2
NX, NY, NZ = 4, 8, 8
ROWS, COLS = 256, 128
GROUPS = 16
CUT = 128
MESH = pl.DeviceIdType.MESH


def place(x, y, z, c):
    return ((x // 2) * NY + y, z * 4 + (x % 2) * 2 + c)


def slot(x, z):
    return z * 4 + (x % 2) * 2 + x // 2


def arrived(ref, sem):
    pltpu.make_async_copy(ref, ref, sem).wait()


def kernel(
    density, pattern, keep_mask, out,
    message, own, panel, column, left, right, total, square, answer, reply,
    swap_sems, panel_sems, column_sems, send_sems,
):
    row, col = lax.axis_index("row"), lax.axis_index("col")
    y, z, c = row % NY, col // 4, col % 2
    h, l = row // NY, (col // 2) % 2
    x = h * 2 + l

    def at(dx=0, dy=0, dz=0, core=None):
        return place(
            (x + dx + NX) % NX, (y + dy + NY) % NY, (z + dz + NZ) % NZ, c if core is None else core
        )

    sibling = at(core=1 - c)
    across = at(dx=2, core=1 - c)
    swaps = h != c
    barrier = pltpu.get_barrier_semaphore()
    friends = [
        at(dx=1), at(dx=-1), at(dx=2), at(dy=1), at(dy=-1), at(dz=1), at(dz=-1), sibling, across,
    ]
    for friend in friends:
        pl.semaphore_signal(barrier, inc=1, device_id=friend, device_id_type=MESH)

    for i in range(2):
        rows = pl.ds(i * 128, 128)
        message[rows, :] = density[rows, :] * pattern[i, 0].astype(jnp.float32)
        message[pl.ds(ROWS + 8 * i, 8), :] = jnp.zeros((8, COLS), jnp.float32) + keep_mask[
            i, 0
        ].astype(jnp.float32)
    pl.semaphore_wait(barrier, len(friends))

    @pl.when(swaps)
    def _():
        swap = pltpu.make_async_remote_copy(
            message, own, swap_sems.at[0], swap_sems.at[1], device_id=across, device_id_type=MESH
        )
        swap.start()
        swap.wait()

    @pl.when(jnp.logical_not(swaps))
    def _():
        own[...] = message[...]

    def split(value):
        high = value.astype(jnp.bfloat16)
        low = (value - high.astype(jnp.float32)).astype(jnp.bfloat16)
        return high, low

    def split_panel(s, zz):
        for i in range(2):
            for j in range(2):
                high, low = split(panel[s, zz * 4 + i * 2 + j])
                left[zz * 2 + i, 0:ROWS, j * 128 : (j + 1) * 128] = high
                left[zz * 2 + i, ROWS : 2 * ROWS, j * 128 : (j + 1) * 128] = low

    def split_column(s, p, g):
        high, low = split(column[s, p, g])
        right[g, :, 0:COLS] = high
        right[g, :, COLS : 2 * COLS] = low

    def multiply(g):
        total[...] += jnp.dot(left[g], right[g], preferred_element_type=jnp.float32)

    def finish(i):
        rows, below = pl.ds(i * 128, 128), pl.ds(ROWS + i * 128, 128)
        one, two = pl.ds(0, COLS), pl.ds(COLS, COLS)
        value = total[rows, one] + (total[rows, two] + total[below, one] + total[below, two])
        return value * own[pl.ds(ROWS + 8 * i, 1), :]

    def step(s, _):
        def send_panel(xx, zz, first, size, half, to):
            part = panel.at[s, slot(xx, zz), pl.ds(first, size)]
            color = first // CUT
            pltpu.make_async_remote_copy(
                part, part, send_sems.at[s, 0], panel_sems.at[s, slot(xx, zz), color * 2 + half],
                device_id=to, device_id_type=MESH,
            ).start()

        def take_panel(xx, zz, first, size, half):
            part = panel.at[s, slot(xx, zz), pl.ds(first, size)]
            arrived(part, panel_sems.at[s, slot(xx, zz), (first // CUT) * 2 + half])

        def send_column(p, cc, yy, first, size, half, to):
            part = column.at[s, p, cc * NY + yy, pl.ds(first, size)]
            pltpu.make_async_remote_copy(
                part, part, send_sems.at[s, 1 + p], column_sems.at[s, p, cc * NY + yy, half],
                device_id=to, device_id_type=MESH,
            ).start()

        def take_column(p, cc, yy, first, size, half):
            part = column.at[s, p, cc * NY + yy, pl.ds(first, size)]
            arrived(part, column_sems.at[s, p, cc * NY + yy, half])

        def wrap(v, n):
            return (v + n) % n

        def column_round(p, d):
            for side in (1, -1):
                yy = wrap(y - side * d, NY)
                half = 0 if side == 1 else 1
                if d < 4:
                    take_column(p, c, yy, 0, ROWS, 0)
                    if d < 3:
                        send_column(p, c, yy, 0, ROWS, 0, at(dy=side))
                    else:
                        send_column(p, c, yy, half * 128, 128, half, at(dy=side))
                    send_column(p, c, yy, 0, ROWS, 0, sibling)
                else:
                    take_column(p, c, yy, half * 128, 128, half)
                    send_column(p, c, yy, half * 128, 128, half, sibling)

        def column_start(p):
            for side in (1, -1):
                send_column(p, c, y, 0, ROWS, 0, at(dy=side))
            send_column(p, c, y, 0, ROWS, 0, sibling)

        def column_other(p, d):
            for side in (1, -1):
                yy = wrap(y - side * d, NY)
                if d < 4:
                    if d > 0 or side == 1:
                        take_column(p, 1 - c, yy, 0, ROWS, 0)
                else:
                    half = 0 if side == 1 else 1
                    take_column(p, 1 - c, yy, half * 128, 128, half)

        def along_x(zz, first, size, half):
            for dx in (2, 1, -1):
                send_panel(x, zz, first, size, half, at(dx=dx))

        def second_round(d):
            for side in (1, -1):
                zz = wrap(z - side * d, NZ)
                half = 0 if side == 1 else 1
                if d < 4:
                    take_panel(x, zz, CUT, 128, 0)
                    if d < 3:
                        send_panel(x, zz, CUT, 128, 0, at(dz=side))
                    else:
                        send_panel(x, zz, CUT + half * 64, 64, half, at(dz=side))
                    along_x(zz, CUT, 128, 0)
                else:
                    take_panel(x, zz, CUT + half * 64, 64, half)
                    along_x(zz, CUT + half * 64, 64, half)

        def first_round(d):
            for dx in (0, 1, -1, 2):
                xx = wrap(x + dx, NX)
                for side in (1, -1):
                    zz = wrap(z - side * d, NZ)
                    half = 0 if side == 1 else 1
                    if d < 4:
                        take_panel(xx, zz, 0, 128, 0)
                        if d < 3:
                            send_panel(xx, zz, 0, 128, 0, at(dz=side))
                        else:
                            send_panel(xx, zz, half * 64, 64, half, at(dz=side))
                    else:
                        take_panel(xx, zz, half * 64, 64, half)

        def panel_ready(d):
            for dx in (1, -1, 2):
                xx = wrap(x + dx, NX)
                for side in (1, -1):
                    zz = wrap(z - side * d, NZ)
                    half = 0 if side == 1 else 1
                    if d == 4:
                        take_panel(xx, zz, CUT + half * 64, 64, half)
                    elif d > 0 or side == 1:
                        take_panel(xx, zz, CUT, 128, 0)
            for side in (1, -1):
                if side == 1 or d in (1, 2, 3):
                    split_panel(s, wrap(z - side * d, NZ))

        def panel_dots(d):
            for side in (1, -1):
                if side == 1 or d in (1, 2, 3):
                    zz = wrap(z - side * d, NZ)
                    for i in range(2):
                        multiply(zz * 2 + i)

        def column_dots(p, cc, d, dots):
            for side in (1, -1):
                if side == 1 or d in (1, 2, 3):
                    g = cc * NY + wrap(y - side * d, NY)
                    split_column(s, p, g)
                    if dots:
                        multiply(g)

        panel[s, slot(x, z)] = own[0:ROWS, :]
        column[s, 0, c * NY + y] = own[0:ROWS, :]
        for side in (1, -1):
            send_panel(x, z, CUT, 128, 0, at(dz=side))
        along_x(z, 0, 128, 0)
        for side in (1, -1):
            send_column(0, c, y, 0, ROWS, 0, at(dy=side))
            send_panel(x, z, 0, 128, 0, at(dz=side))
        along_x(z, CUT, 128, 0)
        send_column(0, c, y, 0, ROWS, 0, sibling)
        total[...] = jnp.zeros_like(total)
        column_dots(0, c, 0, False)

        for dx in (1, -1, 2):
            xx = wrap(x + dx, NX)
            take_panel(xx, z, 0, 128, 0)
            for side in (1, -1):
                send_panel(xx, z, 0, 128, 0, at(dz=side))
        second_round(1)
        column_round(0, 1)
        column_other(0, 0)
        column_dots(0, 1 - c, 0, False)
        column_dots(0, c, 1, False)
        first_round(1)
        column_round(0, 2)
        column_other(0, 1)
        second_round(2)
        column_dots(0, 1 - c, 1, False)
        column_dots(0, c, 2, False)
        panel_ready(0)
        column_round(0, 3)
        column_other(0, 2)
        first_round(2)
        column_dots(0, 1 - c, 2, False)
        column_dots(0, c, 3, False)
        panel_ready(1)
        column_round(0, 4)
        column_other(0, 3)
        second_round(3)
        column_dots(0, 1 - c, 3, False)
        column_dots(0, c, 4, False)
        first_round(3)
        column_other(0, 4)
        column_dots(0, 1 - c, 4, False)
        panel_dots(0)
        panel_dots(1)
        panel_ready(2)
        second_round(4)
        panel_dots(2)
        first_round(4)
        panel_ready(3)
        panel_dots(3)
        panel_ready(4)
        panel_dots(4)

        for i in range(2):
            column[s, 1, c * NY + y, pl.ds(i * 128, 128)] = finish(i)
        column_start(1)
        total[...] = jnp.zeros_like(total)
        column_dots(1, c, 0, True)
        column_round(1, 1)
        column_other(1, 0)
        column_dots(1, 1 - c, 0, True)
        column_dots(1, c, 1, True)
        column_round(1, 2)
        column_other(1, 1)
        column_dots(1, 1 - c, 1, True)
        column_dots(1, c, 2, True)
        column_round(1, 3)
        column_other(1, 2)
        column_dots(1, 1 - c, 2, True)
        column_dots(1, c, 3, True)
        column_round(1, 4)
        column_other(1, 3)
        column_dots(1, 1 - c, 3, True)
        column_dots(1, c, 4, True)
        column_other(1, 4)
        column_dots(1, 1 - c, 4, True)
        for i in range(2):
            rows = pl.ds(i * 128, 128)
            own[rows, :] = 3.0 * column[s, 1, c * NY + y, rows] - 2.0 * finish(i)

        arrived(panel.at[s, pl.ds(0, 31)], send_sems.at[s, 0])
        for p in range(2):
            arrived(column.at[s, p, pl.ds(0, 15)], send_sems.at[s, 1 + p])
        return 0

    lax.fori_loop(0, STEPS, step, 0)

    @pl.when(swaps)
    def _():
        answer[...] = own[0:ROWS, :]
        swap = pltpu.make_async_remote_copy(
            answer, reply, swap_sems.at[2], swap_sems.at[3], device_id=across, device_id_type=MESH
        )
        swap.start()
        swap.wait()
        out[...] = reply[...]

    @pl.when(jnp.logical_not(swaps))
    def _():
        out[...] = own[0:ROWS, :]


def per_device(density, pattern, keep_mask):
    f32, bf16 = jnp.float32, jnp.bfloat16
    return pl.pallas_call(
        kernel,
        out_shape=jax.ShapeDtypeStruct((ROWS, COLS), f32),
        in_specs=[
            pl.BlockSpec(memory_space=pltpu.VMEM),
            pl.BlockSpec(memory_space=pltpu.SMEM),
            pl.BlockSpec(memory_space=pltpu.SMEM),
        ],
        out_specs=pl.BlockSpec(memory_space=pltpu.VMEM),
        scratch_shapes=[
            pltpu.VMEM((ROWS + 16, COLS), f32),
            pltpu.VMEM((ROWS + 16, COLS), f32),
            pltpu.VMEM((STEPS, 32, ROWS, COLS), f32),
            pltpu.VMEM((STEPS, 2, GROUPS, ROWS, COLS), f32),
            pltpu.VMEM((GROUPS, 2 * ROWS, 2 * COLS), bf16),
            pltpu.VMEM((GROUPS, ROWS, 2 * COLS), bf16),
            pltpu.VMEM((2 * ROWS, 2 * COLS), f32),
            pltpu.VMEM((ROWS, COLS), f32),
            pltpu.VMEM((ROWS, COLS), f32),
            pltpu.VMEM((ROWS, COLS), f32),
            pltpu.SemaphoreType.DMA((4,)),
            pltpu.SemaphoreType.DMA((STEPS, 32, 4)),
            pltpu.SemaphoreType.DMA((STEPS, 2, GROUPS, 2)),
            pltpu.SemaphoreType.DMA((STEPS, 3)),
        ],
        compiler_params=pltpu.CompilerParams(
            collective_id=0, has_side_effects=True, vmem_limit_bytes=40 << 20
        ),
        cost_estimate=pl.CostEstimate(
            flops=2 * STEPS * 2 * ROWS * 4096 * COLS, bytes_accessed=1 << 18, transcendentals=0
        ),
    )(density, pattern, keep_mask)


def solution(mesh):
    placed = (P("row", "col"), P("row", "col"), P("row", "col"))
    return jax.shard_map(
        per_device, mesh=mesh, in_specs=placed, out_specs=P("row", "col"), check_vma=False
    )
```

```python
import jax
import jax.numpy as jnp
from jax import lax
from jax.experimental import pallas as pl
from jax.experimental.pallas import tpu as pltpu
from jax.sharding import PartitionSpec as P

STEPS = 2
NX, NY, NZ = 4, 8, 8
RING = 8
ROWS, COLS = 256, 128
GROUPS = 16
FIRST = (192, 192, 128)
MESH = pl.DeviceIdType.MESH
PANEL, COLUMN, SQUARE = 0, 1, 2


def pieces(first):
    half, rest = first // 2, (ROWS - first) // 2
    cut = [(0, half, True, 1), (half, half, True, -1)]
    if rest:
        cut += [(first, rest, False, 1), (first + rest, rest, False, -1)]
    return cut


def place(x, y, z, c):
    return ((x // 2) * NY + y, z * 4 + (x % 2) * 2 + c)


def arrived(ref, sem):
    pltpu.make_async_copy(ref, ref, sem).wait()


def kernel(
    density, pattern, keep_mask, out,
    own, panel, column, left, right, total, panel_sems, column_sems, send_sems,
):
    row, col = lax.axis_index("row"), lax.axis_index("col")
    y, z, c = row % NY, col // 4, col % 2
    h, l = row // NY, (col // 2) % 2
    x = h * 2 + l

    def at(dx=0, dy=0, dz=0, core=None):
        return place(
            (x + dx + NX) % NX, (y + dy + NY) % NY, (z + dz + NZ) % NZ, c if core is None else core
        )

    sibling = at(core=1 - c)
    across = at(dx=2)
    beside = at(dx=1 - 2 * l)
    barrier = pltpu.get_barrier_semaphore()
    friends = [across, beside, at(dy=1), at(dy=-1), at(dz=1), at(dz=-1), sibling]
    for friend in friends:
        pl.semaphore_signal(barrier, inc=1, device_id=friend, device_id_type=MESH)
    for i in range(2):
        rows = pl.ds(i * 128, 128)
        own[rows, :] = density[rows, :] * pattern[i, 0].astype(jnp.float32)
    pl.semaphore_wait(barrier, len(friends))

    def split(value):
        high = value.astype(jnp.bfloat16)
        low = (value - high.astype(jnp.float32)).astype(jnp.bfloat16)
        return high, low

    def finish(i):
        rows, below = pl.ds(i * 128, 128), pl.ds(ROWS + i * 128, 128)
        one, two = pl.ds(0, COLS), pl.ds(COLS, COLS)
        value = total[rows, one] + (total[rows, two] + total[below, one] + total[below, two])
        return value * keep_mask[i, 0].astype(jnp.float32)

    def multiply(g):
        total[...] += jnp.dot(left[g], right[g], preferred_element_type=jnp.float32)

    def step(s, _):
        def slot(kind, w, pos, core):
            if kind == PANEL:
                return pos * 4 + (l if w == 0 else 1 - l) * 2 + core
            return (h if w == 0 else 1 - h) * NY + pos

        def place_of(kind, w, pos, piece, core):
            first, size, _, _ = piece
            n = slot(kind, w, pos, core)
            k = pieces(FIRST[kind]).index(piece)
            if kind == PANEL:
                return panel.at[s, n, pl.ds(first, size)], panel_sems.at[s, n, k]
            return column.at[s, kind - 1, n, pl.ds(first, size)], column_sems.at[s, kind - 1, n, k]

        def send(kind, w, pos, piece, to):
            part, sem = place_of(kind, w, pos, piece, c)
            pltpu.make_async_remote_copy(
                part, part, send_sems.at[s, kind], sem, device_id=to, device_id_type=MESH
            ).start()

        def take(kind, w, pos, piece, core):
            arrived(*place_of(kind, w, pos, piece, core))

        def me(kind):
            return z if kind == PANEL else y

        def pos_of(kind, d, side):
            return (me(kind) - side * d + RING) % RING

        def onward(kind, side):
            return at(dz=side) if kind == PANEL else at(dy=side)

        def partner(kind):
            return beside if kind == PANEL else across

        def share(kind, w, pos, piece):
            if kind == PANEL:
                send(kind, w, pos, piece, sibling)

        def begin(kind):
            cut = pieces(FIRST[kind])
            for piece in cut:
                if piece[2]:
                    send(kind, 0, me(kind), piece, partner(kind))
            for piece in cut[::-1]:
                for side in (1, -1):
                    send(kind, 0, me(kind), piece, onward(kind, side))

        def begin_late(kind):
            for piece in pieces(FIRST[kind]):
                if not piece[2]:
                    send(kind, 0, me(kind), piece, partner(kind))

        def from_partner(kind):
            for piece in pieces(FIRST[kind]):
                if piece[2]:
                    take(kind, 1, me(kind), piece, c)
                    for side in (1, -1):
                        send(kind, 1, me(kind), piece, onward(kind, side))
                    share(kind, 1, me(kind), piece)

        def ring(kind, w, d):
            cut = pieces(FIRST[kind])
            for piece in cut[::-1] if w == 0 else cut[:2]:
                for side in (1, -1):
                    pos = pos_of(kind, d, side)
                    far = side == piece[3]
                    if d < 4 or far:
                        take(kind, w, pos, piece, c)
                        if d < 3 or (d == 3 and far):
                            send(kind, w, pos, piece, onward(kind, side))
                        if not piece[2]:
                            send(kind, w, pos, piece, partner(kind))
                        share(kind, w, pos, piece)

        def sides(d):
            return (1, -1) if d in (1, 2, 3) else (1,)

        def exchanged(kind, d):
            for piece in pieces(FIRST[kind])[2:]:
                for side in sides(d):
                    pos = pos_of(kind, d, side)
                    take(kind, 1, pos, piece, c)
                    share(kind, 1, pos, piece)

        def shared(d):
            for w in range(2):
                for side in sides(d):
                    for piece in pieces(FIRST[PANEL]):
                        take(PANEL, w, pos_of(PANEL, d, side), piece, 1 - c)

        def split_panel(d):
            for side in sides(d):
                zz = pos_of(PANEL, d, side)
                for i in range(2):
                    for j in range(2):
                        high, low = split(panel[s, zz * 4 + i * 2 + j])
                        left[zz * 2 + i, 0:ROWS, j * COLS : (j + 1) * COLS] = high
                        left[zz * 2 + i, ROWS : 2 * ROWS, j * COLS : (j + 1) * COLS] = low

        def split_column(kind, w, d, dots):
            for side in sides(d):
                g = slot(kind, w, pos_of(kind, d, side), c)
                high, low = split(column[s, kind - 1, g])
                right[g, :, 0:COLS] = high
                right[g, :, COLS : 2 * COLS] = low
                if dots:
                    multiply(g)

        def distance(a, b):
            apart = (a - b + RING) % RING
            return jnp.minimum(apart, RING - apart)

        def dots(low, high):
            def one(g, _):
                last = jnp.maximum(distance(g // 2, z), distance(g % NY, y))

                @pl.when(jnp.logical_and(last >= low, last <= high))
                def _():
                    multiply(g)

                return 0

            lax.fori_loop(0, GROUPS, one, 0)

        both = (PANEL, COLUMN)
        panel[s, col] = own[...]
        column[s, 0, row] = own[...]
        for kind in both:
            begin(kind)
        for piece in pieces(FIRST[PANEL]):
            share(PANEL, 0, z, piece)
        total[...] = jnp.zeros_like(total)
        split_column(COLUMN, 0, 0, False)

        def each(function, *args):
            for kind in both:
                function(kind, *args)

        each(ring, 0, 1)
        each(from_partner)
        each(begin_late)
        split_column(COLUMN, 0, 1, False)
        each(ring, 0, 2)
        each(ring, 1, 1)
        each(exchanged, 0)
        each(exchanged, 1)
        split_column(COLUMN, 1, 0, False)
        split_column(COLUMN, 1, 1, False)
        shared(0)
        split_panel(0)
        each(ring, 0, 3)
        each(ring, 1, 2)
        each(exchanged, 2)
        split_column(COLUMN, 0, 2, False)
        split_column(COLUMN, 1, 2, False)
        shared(1)
        split_panel(1)
        each(ring, 0, 4)
        each(ring, 1, 3)
        each(exchanged, 3)
        split_column(COLUMN, 0, 3, False)
        split_column(COLUMN, 1, 3, False)
        shared(2)
        split_panel(2)
        dots(0, 2)
        each(ring, 1, 4)
        each(exchanged, 4)
        split_column(COLUMN, 0, 4, False)
        shared(3)
        split_panel(3)
        dots(3, 3)
        split_column(COLUMN, 1, 4, False)
        shared(4)
        split_panel(4)
        dots(4, 4)

        for i in range(2):
            column[s, 1, row, pl.ds(i * 128, 128)] = finish(i)
        begin(SQUARE)
        total[...] = jnp.zeros_like(total)
        split_column(SQUARE, 0, 0, True)
        ring(SQUARE, 0, 1)
        from_partner(SQUARE)
        begin_late(SQUARE)
        split_column(SQUARE, 0, 1, True)
        ring(SQUARE, 0, 2)
        ring(SQUARE, 1, 1)
        exchanged(SQUARE, 0)
        exchanged(SQUARE, 1)
        split_column(SQUARE, 1, 0, True)
        split_column(SQUARE, 1, 1, True)
        ring(SQUARE, 0, 3)
        ring(SQUARE, 1, 2)
        exchanged(SQUARE, 2)
        split_column(SQUARE, 0, 2, True)
        split_column(SQUARE, 1, 2, True)
        ring(SQUARE, 0, 4)
        ring(SQUARE, 1, 3)
        exchanged(SQUARE, 3)
        split_column(SQUARE, 0, 3, True)
        split_column(SQUARE, 1, 3, True)
        split_column(SQUARE, 0, 4, True)
        ring(SQUARE, 1, 4)
        exchanged(SQUARE, 4)
        split_column(SQUARE, 1, 4, True)
        for i in range(2):
            rows = pl.ds(i * 128, 128)
            own[rows, :] = 3.0 * column[s, 1, row, rows] - 2.0 * finish(i)

        arrived(panel.at[s, pl.ds(0, 31)], send_sems.at[s, PANEL])
        for p in range(2):
            arrived(column.at[s, p, pl.ds(0, 15)], send_sems.at[s, 1 + p])
        return 0

    lax.fori_loop(0, STEPS, step, 0)
    out[...] = own[...]


def per_device(density, pattern, keep_mask):
    f32, bf16 = jnp.float32, jnp.bfloat16
    return pl.pallas_call(
        kernel,
        out_shape=jax.ShapeDtypeStruct((ROWS, COLS), f32),
        in_specs=[
            pl.BlockSpec(memory_space=pltpu.VMEM),
            pl.BlockSpec(memory_space=pltpu.SMEM),
            pl.BlockSpec(memory_space=pltpu.SMEM),
        ],
        out_specs=pl.BlockSpec(memory_space=pltpu.VMEM),
        scratch_shapes=[
            pltpu.VMEM((ROWS, COLS), f32),
            pltpu.VMEM((STEPS, 32, ROWS, COLS), f32),
            pltpu.VMEM((STEPS, 2, GROUPS, ROWS, COLS), f32),
            pltpu.VMEM((GROUPS, 2 * ROWS, 2 * COLS), bf16),
            pltpu.VMEM((GROUPS, ROWS, 2 * COLS), bf16),
            pltpu.VMEM((2 * ROWS, 2 * COLS), f32),
            pltpu.SemaphoreType.DMA((STEPS, 32, 4)),
            pltpu.SemaphoreType.DMA((STEPS, 2, GROUPS, 4)),
            pltpu.SemaphoreType.DMA((STEPS, 3)),
        ],
        compiler_params=pltpu.CompilerParams(
            collective_id=0, has_side_effects=True, vmem_limit_bytes=40 << 20
        ),
        cost_estimate=pl.CostEstimate(
            flops=2 * STEPS * 2 * ROWS * 4096 * COLS, bytes_accessed=1 << 18, transcendentals=0
        ),
    )(density, pattern, keep_mask)


def solution(mesh):
    placed = (P("row", "col"), P("row", "col"), P("row", "col"))
    return jax.shard_map(
        per_device, mesh=mesh, in_specs=placed, out_specs=P("row", "col"), check_vma=False
    )
```

```python
import functools

import jax
import jax.numpy as jnp
from jax import lax
from jax.experimental import pallas as pl
from jax.experimental.pallas import tpu as pltpu
from jax.sharding import PartitionSpec as P

STEPS = 2
NX, NY, NZ = 4, 8, 8
RING = 8
ROWS, COLS = 256, 128
GROUPS = 16
MESH = pl.DeviceIdType.MESH
PANEL, COLUMN, SQUARE = 0, 1, 2
CHUNK = 64
MOST = ((False, 1), (True, -1), (True, 1), (True, -1))
HALF = ((False, 1), (False, -1), (True, 1), (True, -1))
ROUTES = (MOST, MOST, HALF)


def place(x, y, z, c):
    return ((x // 2) * NY + y, z * 4 + (x % 2) * 2 + c)


def arrived(ref, sem):
    pltpu.make_async_copy(ref, ref, sem).wait()


def kernel(
    density, pattern, keep_mask, out,
    own, panel, column, left, right, total, panel_sems, column_sems, send_sems, load_sem,
):
    row, col = lax.axis_index("row"), lax.axis_index("col")
    y, z, c = row % NY, col // 4, col % 2
    h, l = row // NY, (col // 2) % 2
    x = h * 2 + l

    def at(dx=0, dy=0, dz=0, core=None):
        return place(
            (x + dx + NX) % NX, (y + dy + NY) % NY, (z + dz + NZ) % NZ, c if core is None else core
        )

    sibling = at(core=1 - c)
    across = at(dx=2)
    beside = at(dx=1 - 2 * l)
    barrier = pltpu.get_barrier_semaphore()
    friends = [across, beside, at(dy=1), at(dy=-1), at(dz=1), at(dz=-1), sibling]
    for friend in friends:
        pl.semaphore_signal(barrier, inc=1, device_id=friend, device_id_type=MESH)
    load = pltpu.make_async_copy(density, own, load_sem)
    load.start()
    pl.semaphore_wait(barrier, len(friends))
    load.wait()
    for i in range(2):
        rows = pl.ds(i * 128, 128)
        own[rows, :] *= pattern[0, i].astype(jnp.float32)

    def split(value):
        high = value.astype(jnp.bfloat16)
        low = (value - high.astype(jnp.float32)).astype(jnp.bfloat16)
        return high, low

    def rows_of(r):
        return pl.ds(r * CHUNK, CHUNK)

    def multiply(g):
        both = left[g].reshape(2 * ROWS, 2 * COLS)
        total[...] += jnp.dot(both, right[g], preferred_element_type=jnp.float32)

    def clear():
        total[...] = jnp.zeros_like(total)

    def product(r, groups, begun):
        both = total[pl.ds(r * 2 * CHUNK, 2 * CHUNK), :] if begun else 0.0
        for g in groups:
            both += jnp.dot(left[g, r], right[g], preferred_element_type=jnp.float32)
        high, low = both[0:CHUNK], both[CHUNK : 2 * CHUNK]
        value = high[:, 0:COLS] + (high[:, COLS : 2 * COLS] + low[:, 0:COLS] + low[:, COLS : 2 * COLS])
        return value * keep_mask[0, r // 2].astype(jnp.float32)

    def slot(kind, w, pos, core):
        if kind == PANEL:
            return pos * 4 + (l if w == 0 else 1 - l) * 2 + core
        return (h if w == 0 else 1 - h) * NY + pos

    def place_of(s, kind, w, pos, r, core):
        n = slot(kind, w, pos, core)
        if kind == PANEL:
            return panel.at[s, n, rows_of(r)], panel_sems.at[s, n, r]
        return column.at[s, kind - 1, n, rows_of(r)], column_sems.at[s, kind - 1, n, r]

    def send(s, kind, w, pos, r, to):
        part, sem = place_of(s, kind, w, pos, r, c)
        pltpu.make_async_remote_copy(
            part, part, send_sems.at[s, kind], sem, device_id=to, device_id_type=MESH
        ).start()

    def me(kind):
        return z if kind == PANEL else y

    def onward(kind, side):
        return at(dz=side) if kind == PANEL else at(dy=side)

    def partner(kind):
        return beside if kind == PANEL else across

    def share(s, kind, w, pos, r):
        if kind == PANEL:
            send(s, kind, w, pos, r, sibling)

    def launch(s, kind, r):
        along_x, far = ROUTES[kind][r]
        send(s, kind, 0, me(kind), r, onward(kind, far))
        if along_x:
            send(s, kind, 0, me(kind), r, partner(kind))
        send(s, kind, 0, me(kind), r, onward(kind, -far))
        share(s, kind, 0, me(kind), r)

    def launch_current(s, r):
        panel[s, col, rows_of(r)] = own[rows_of(r), :]
        column[s, 0, row, rows_of(r)] = own[rows_of(r), :]
        launch(s, PANEL, r)
        launch(s, COLUMN, r)

    for r in range(4):
        launch_current(0, r)

    def step(s, _):
        def take(kind, w, pos, r, core):
            arrived(*place_of(s, kind, w, pos, r, core))

        def pos_of(kind, d, side):
            return (me(kind) - side * d + RING) % RING

        def late(kind):
            for r in range(4):
                if not ROUTES[kind][r][0]:
                    send(s, kind, 0, me(kind), r, partner(kind))

        def sides(d):
            return (1, -1) if d in (1, 2, 3) else (1,)

        def ring(kind, w, d, r):
            along_x, far = ROUTES[kind][r]
            if d == 0:
                take(kind, w, me(kind), r, c)
                for side in (far, -far):
                    send(s, kind, w, me(kind), r, onward(kind, side))
                share(s, kind, w, me(kind), r)
                return
            for side in (far, -far):
                pos = pos_of(kind, d, side)
                if d < 4 or side == far:
                    take(kind, w, pos, r, c)
                    if d < 3 or (d == 3 and side == far):
                        send(s, kind, w, pos, r, onward(kind, side))
                    if not along_x:
                        send(s, kind, w, pos, r, partner(kind))
                    share(s, kind, w, pos, r)

        def turn(kinds, d, work=()):
            work = list(work)
            for r in range(4):
                for kind in kinds:
                    if d <= 4:
                        ring(kind, 0, d, r)
                    if ROUTES[kind][r][0]:
                        ring(kind, 1, d - 1, r)
                    if work:
                        work.pop(0)()
            for unit in work:
                unit()
            if d == 1:
                for kind in kinds:
                    late(kind)

        def exchanged(kinds, d):
            for r in range(4):
                for kind in kinds:
                    if not ROUTES[kind][r][0]:
                        for side in sides(d):
                            pos = pos_of(kind, d, side)
                            take(kind, 1, pos, r, c)
                            share(s, kind, 1, pos, r)

        def shared(d):
            for w in range(2):
                for side in sides(d):
                    for r in range(4):
                        take(PANEL, w, pos_of(PANEL, d, side), r, 1 - c)

        def split_block(zz, i, j):
            high, low = split(panel[s, zz * 4 + i * 2 + j])
            for r in range(4):
                rows = slice(r * CHUNK, (r + 1) * CHUNK)
                left[zz * 2 + i, r, 0:CHUNK, j * COLS : (j + 1) * COLS] = high[rows]
                left[zz * 2 + i, r, CHUNK : 2 * CHUNK, j * COLS : (j + 1) * COLS] = low[rows]

        def panel_work(d):
            return [
                functools.partial(split_block, pos_of(PANEL, d, side), i, j)
                for side in sides(d) for i in range(2) for j in range(2)
            ]

        def column_work(kind, w, d):
            return [functools.partial(split_one, kind, w, d, side) for side in sides(d)]

        def run(work):
            for unit in work:
                unit()

        def split_one(kind, w, d, side):
            g = slot(kind, w, pos_of(kind, d, side), c)
            high, low = split(column[s, kind - 1, g])
            right[g, :, 0:COLS] = high
            right[g, :, COLS : 2 * COLS] = low
            if kind == SQUARE and d < 4:
                multiply(g)

        both = (PANEL, COLUMN)
        turn(both, 1, column_work(COLUMN, 0, 0))
        turn(both, 2, column_work(COLUMN, 0, 1))
        exchanged(both, 0)
        shared(0)
        turn(both, 3, panel_work(0) + column_work(COLUMN, 0, 2) + column_work(COLUMN, 1, 0))
        exchanged(both, 1)
        shared(1)
        turn(both, 4, panel_work(1) + column_work(COLUMN, 1, 1))
        exchanged(both, 2)
        shared(2)
        turn(both, 5, panel_work(2) + column_work(COLUMN, 0, 3) + column_work(COLUMN, 1, 2))
        exchanged(both, 3)
        run(column_work(COLUMN, 0, 4) + column_work(COLUMN, 1, 3))
        exchanged(both, 4)
        shared(3)
        run(panel_work(3) + column_work(COLUMN, 1, 4))
        shared(4)
        run(panel_work(4))

        for r in range(4):
            column[s, 1, row, rows_of(r)] = product(r, range(GROUPS), False)
            launch(s, SQUARE, r)
        only = (SQUARE,)
        clear()
        turn(only, 1, column_work(SQUARE, 0, 0))
        turn(only, 2, column_work(SQUARE, 0, 1))
        exchanged(only, 0)
        turn(only, 3, column_work(SQUARE, 0, 2) + column_work(SQUARE, 1, 0))
        exchanged(only, 1)
        turn(only, 4, column_work(SQUARE, 0, 3) + column_work(SQUARE, 1, 1))
        exchanged(only, 2)
        turn(only, 5, column_work(SQUARE, 1, 2))
        exchanged(only, 3)
        run(column_work(SQUARE, 1, 3) + column_work(SQUARE, 0, 4))
        exchanged(only, 4)
        run(column_work(SQUARE, 1, 4))
        last = [slot(SQUARE, w, pos_of(SQUARE, 4, 1), c) for w in range(2)]
        for r in range(4):
            own[rows_of(r), :] = 3.0 * column[s, 1, row, rows_of(r)] - 2.0 * product(r, last, True)

            @pl.when(s + 1 < STEPS)
            def _():
                launch_current(s + 1, r)

        arrived(panel.at[s, pl.ds(0, 31)], send_sems.at[s, PANEL])
        for p in range(2):
            arrived(column.at[s, p, pl.ds(0, 15)], send_sems.at[s, 1 + p])
        return 0

    lax.fori_loop(0, STEPS, step, 0)
    out[...] = own[...]


def per_device(density, pattern, keep_mask):
    f32, bf16 = jnp.float32, jnp.bfloat16
    return pl.pallas_call(
        kernel,
        out_shape=jax.ShapeDtypeStruct((ROWS, COLS), f32),
        in_specs=[
            pl.BlockSpec(memory_space=pltpu.HBM),
            pl.BlockSpec(memory_space=pltpu.SMEM),
            pl.BlockSpec(memory_space=pltpu.SMEM),
        ],
        out_specs=pl.BlockSpec(memory_space=pltpu.VMEM),
        scratch_shapes=[
            pltpu.VMEM((ROWS, COLS), f32),
            pltpu.VMEM((STEPS, 32, ROWS, COLS), f32),
            pltpu.VMEM((STEPS, 2, GROUPS, ROWS, COLS), f32),
            pltpu.VMEM((GROUPS, 4, 2 * CHUNK, 2 * COLS), bf16),
            pltpu.VMEM((GROUPS, ROWS, 2 * COLS), bf16),
            pltpu.VMEM((2 * ROWS, 2 * COLS), f32),
            pltpu.SemaphoreType.DMA((STEPS, 32, 4)),
            pltpu.SemaphoreType.DMA((STEPS, 2, GROUPS, 4)),
            pltpu.SemaphoreType.DMA((STEPS, 3)),
            pltpu.SemaphoreType.DMA,
        ],
        compiler_params=pltpu.CompilerParams(
            collective_id=0, has_side_effects=True, vmem_limit_bytes=40 << 20
        ),
        cost_estimate=pl.CostEstimate(
            flops=2 * STEPS * 2 * ROWS * 4096 * COLS, bytes_accessed=1 << 18, transcendentals=0
        ),
    )(density, pattern.T, keep_mask.T)


def solution(mesh):
    placed = (P("row", "col"), P("row", "col"), P("row", "col"))
    return jax.shard_map(
        per_device, mesh=mesh, in_specs=placed, out_specs=P("row", "col"), check_vma=False
    )
```

```python
import functools

import jax
import jax.numpy as jnp
from jax import lax
from jax.experimental import pallas as pl
from jax.experimental.pallas import tpu as pltpu
from jax.sharding import PartitionSpec as P

STEPS = 2
NX, NY, NZ = 4, 8, 8
RING = 8
ROWS, COLS = 256, 128
GROUPS = 16
MESH = pl.DeviceIdType.MESH
PANEL, COLUMN, SQUARE = 0, 1, 2
CHUNK = 64
MOST = ((False, 1), (True, -1), (True, 1), (True, -1))
HALF = ((False, 1), (False, -1), (True, 1), (True, -1))
ROUTES = (MOST, MOST, HALF)


def place(x, y, z, c):
    return ((x // 2) * NY + y, z * 4 + (x % 2) * 2 + c)


def arrived(ref, sem):
    pltpu.make_async_copy(ref, ref, sem).wait()


def kernel(
    density, pattern, keep_mask, out,
    own, panel, column, left, right, total, panel_sems, column_sems, send_sems, load_sem,
):
    row, col = lax.axis_index("row"), lax.axis_index("col")
    y, z, c = row % NY, col // 4, col % 2
    h, l = row // NY, (col // 2) % 2
    x = h * 2 + l

    def at(dx=0, dy=0, dz=0, core=None):
        return place(
            (x + dx + NX) % NX, (y + dy + NY) % NY, (z + dz + NZ) % NZ, c if core is None else core
        )

    sibling = at(core=1 - c)
    across = at(dx=2)
    beside = at(dx=1 - 2 * l)
    barrier = pltpu.get_barrier_semaphore()
    friends = [across, beside, at(dy=1), at(dy=-1), at(dz=1), at(dz=-1), sibling]
    for friend in friends:
        pl.semaphore_signal(barrier, inc=1, device_id=friend, device_id_type=MESH)
    load = pltpu.make_async_copy(density, own, load_sem)
    load.start()
    pl.semaphore_wait(barrier, len(friends))
    load.wait()
    for i in range(2):
        rows = pl.ds(i * 128, 128)
        own[rows, :] *= pattern[0, i].astype(jnp.float32)

    def split(value):
        high = value.astype(jnp.bfloat16)
        low = (value - high.astype(jnp.float32)).astype(jnp.bfloat16)
        return high, low

    def rows_of(r):
        return pl.ds(r * CHUNK, CHUNK)

    def multiply(g):
        both = left[g].reshape(2 * ROWS, 2 * COLS)
        total[...] += jnp.dot(both, right[g], preferred_element_type=jnp.float32)

    def clear():
        total[...] = jnp.zeros_like(total)

    def product(r, groups, begun):
        both = total[pl.ds(r * 2 * CHUNK, 2 * CHUNK), :] if begun else 0.0
        for g in groups:
            both += jnp.dot(left[g, r], right[g], preferred_element_type=jnp.float32)
        high, low = both[0:CHUNK], both[CHUNK : 2 * CHUNK]
        value = high[:, 0:COLS] + (high[:, COLS : 2 * COLS] + low[:, 0:COLS] + low[:, COLS : 2 * COLS])
        return value * keep_mask[0, r // 2].astype(jnp.float32)

    def slot(kind, w, pos, core):
        if kind == PANEL:
            return pos * 4 + (l if w == 0 else 1 - l) * 2 + core
        return (h if w == 0 else 1 - h) * NY + pos

    def place_of(s, kind, w, pos, r, core):
        n = slot(kind, w, pos, core)
        if kind == PANEL:
            return panel.at[s, n, rows_of(r)], panel_sems.at[s, n, r]
        return column.at[s, kind - 1, n, rows_of(r)], column_sems.at[s, kind - 1, n, r]

    def send(s, kind, w, pos, r, to):
        part, sem = place_of(s, kind, w, pos, r, c)
        pltpu.make_async_remote_copy(
            part, part, send_sems.at[s, kind], sem, device_id=to, device_id_type=MESH
        ).start()

    def me(kind):
        return z if kind == PANEL else y

    def onward(kind, side):
        return at(dz=side) if kind == PANEL else at(dy=side)

    def partner(kind):
        return beside if kind == PANEL else across

    def share(s, kind, w, pos, r):
        if kind == PANEL:
            send(s, kind, w, pos, r, sibling)

    def launch(s, kind, r):
        along_x, far = ROUTES[kind][r]
        send(s, kind, 0, me(kind), r, onward(kind, far))
        if along_x:
            send(s, kind, 0, me(kind), r, partner(kind))
        send(s, kind, 0, me(kind), r, onward(kind, -far))
        share(s, kind, 0, me(kind), r)

    def launch_current(s, r):
        panel[s, col, rows_of(r)] = own[rows_of(r), :]
        column[s, 0, row, rows_of(r)] = own[rows_of(r), :]
        launch(s, PANEL, r)
        launch(s, COLUMN, r)

    for r in range(4):
        launch_current(0, r)

    def step(s, _):
        def take(kind, w, pos, r, core):
            arrived(*place_of(s, kind, w, pos, r, core))

        def pos_of(kind, d, side):
            return (me(kind) - side * d + RING) % RING

        def late(kind):
            for r in range(4):
                if not ROUTES[kind][r][0]:
                    send(s, kind, 0, me(kind), r, partner(kind))

        def sides(d):
            return (1, -1) if d in (1, 2, 3) else (1,)

        def ring(kind, w, d, r):
            along_x, far = ROUTES[kind][r]
            if d == 0:
                take(kind, w, me(kind), r, c)
                for side in (far, -far):
                    send(s, kind, w, me(kind), r, onward(kind, side))
                share(s, kind, w, me(kind), r)
                return
            for side in (far, -far):
                pos = pos_of(kind, d, side)
                if d < 4 or side == far:
                    take(kind, w, pos, r, c)
                    if d < 3 or (d == 3 and side == far):
                        send(s, kind, w, pos, r, onward(kind, side))
                    if not along_x:
                        send(s, kind, w, pos, r, partner(kind))
                    share(s, kind, w, pos, r)

        def turn(kinds, d, work=()):
            work = list(work)
            for r in range(4):
                for kind in kinds:
                    if d <= 4:
                        ring(kind, 0, d, r)
                for kind in kinds:
                    if ROUTES[kind][r][0]:
                        ring(kind, 1, d - 1, r)
                    if work:
                        work.pop(0)()
            for unit in work:
                unit()
            if d == 1:
                for kind in kinds:
                    late(kind)

        def exchanged(kinds, d):
            for r in range(4):
                for kind in kinds:
                    if not ROUTES[kind][r][0]:
                        for side in sides(d):
                            pos = pos_of(kind, d, side)
                            take(kind, 1, pos, r, c)
                            share(s, kind, 1, pos, r)

        def shared(d):
            for w in range(2):
                for side in sides(d):
                    for r in range(4):
                        take(PANEL, w, pos_of(PANEL, d, side), r, 1 - c)

        def split_block(zz, i, j):
            high, low = split(panel[s, zz * 4 + i * 2 + j])
            for r in range(4):
                rows = slice(r * CHUNK, (r + 1) * CHUNK)
                left[zz * 2 + i, r, 0:CHUNK, j * COLS : (j + 1) * COLS] = high[rows]
                left[zz * 2 + i, r, CHUNK : 2 * CHUNK, j * COLS : (j + 1) * COLS] = low[rows]

        def panel_work(d):
            return [
                functools.partial(split_block, pos_of(PANEL, d, side), i, j)
                for side in sides(d) for i in range(2) for j in range(2)
            ]

        def column_work(kind, w, d):
            return [functools.partial(split_one, kind, w, d, side) for side in sides(d)]

        def run(work):
            for unit in work:
                unit()

        def split_one(kind, w, d, side):
            g = slot(kind, w, pos_of(kind, d, side), c)
            high, low = split(column[s, kind - 1, g])
            right[g, :, 0:COLS] = high
            right[g, :, COLS : 2 * COLS] = low
            if kind == SQUARE and d < 3:
                multiply(g)

        both = (PANEL, COLUMN)
        turn(both, 1, column_work(COLUMN, 0, 0))
        turn(both, 2, column_work(COLUMN, 0, 1))
        exchanged(both, 0)
        shared(0)
        turn(both, 3, panel_work(0) + column_work(COLUMN, 0, 2) + column_work(COLUMN, 1, 0))
        exchanged(both, 1)
        shared(1)
        turn(both, 4, panel_work(1) + column_work(COLUMN, 1, 1))
        exchanged(both, 2)
        shared(2)
        turn(both, 5, panel_work(2) + column_work(COLUMN, 0, 3) + column_work(COLUMN, 1, 2))
        exchanged(both, 3)
        run(column_work(COLUMN, 0, 4) + column_work(COLUMN, 1, 3))
        exchanged(both, 4)
        shared(3)
        run(panel_work(3) + column_work(COLUMN, 1, 4))
        shared(4)
        run(panel_work(4))

        for r in range(4):
            column[s, 1, row, rows_of(r)] = product(r, range(GROUPS), False)
            launch(s, SQUARE, r)
        only = (SQUARE,)
        clear()
        turn(only, 1, column_work(SQUARE, 0, 0))
        turn(only, 2, column_work(SQUARE, 0, 1))
        exchanged(only, 0)
        turn(only, 3, column_work(SQUARE, 0, 2) + column_work(SQUARE, 1, 0))
        exchanged(only, 1)
        turn(only, 4, column_work(SQUARE, 0, 3) + column_work(SQUARE, 1, 1))
        exchanged(only, 2)
        turn(only, 5, column_work(SQUARE, 1, 2))
        exchanged(only, 3)
        run(column_work(SQUARE, 1, 3) + column_work(SQUARE, 0, 4))
        exchanged(only, 4)
        run(column_work(SQUARE, 1, 4))
        last = [slot(SQUARE, w, pos_of(SQUARE, d, side), c) for d in range(3, 5) for side in sides(d) for w in range(2)]
        for r in range(4):
            own[rows_of(r), :] = 3.0 * column[s, 1, row, rows_of(r)] - 2.0 * product(r, last, True)

            @pl.when(s + 1 < STEPS)
            def _():
                launch_current(s + 1, r)

        arrived(panel.at[s, pl.ds(0, 31)], send_sems.at[s, PANEL])
        for p in range(2):
            arrived(column.at[s, p, pl.ds(0, 15)], send_sems.at[s, 1 + p])
        return 0

    lax.fori_loop(0, STEPS, step, 0)
    out[...] = own[...]


def per_device(density, pattern, keep_mask):
    f32, bf16 = jnp.float32, jnp.bfloat16
    return pl.pallas_call(
        kernel,
        out_shape=jax.ShapeDtypeStruct((ROWS, COLS), f32),
        in_specs=[
            pl.BlockSpec(memory_space=pltpu.HBM),
            pl.BlockSpec(memory_space=pltpu.SMEM),
            pl.BlockSpec(memory_space=pltpu.SMEM),
        ],
        out_specs=pl.BlockSpec(memory_space=pltpu.VMEM),
        scratch_shapes=[
            pltpu.VMEM((ROWS, COLS), f32),
            pltpu.VMEM((STEPS, 32, ROWS, COLS), f32),
            pltpu.VMEM((STEPS, 2, GROUPS, ROWS, COLS), f32),
            pltpu.VMEM((GROUPS, 4, 2 * CHUNK, 2 * COLS), bf16),
            pltpu.VMEM((GROUPS, ROWS, 2 * COLS), bf16),
            pltpu.VMEM((2 * ROWS, 2 * COLS), f32),
            pltpu.SemaphoreType.DMA((STEPS, 32, 4)),
            pltpu.SemaphoreType.DMA((STEPS, 2, GROUPS, 4)),
            pltpu.SemaphoreType.DMA((STEPS, 3)),
            pltpu.SemaphoreType.DMA,
        ],
        compiler_params=pltpu.CompilerParams(
            collective_id=0, has_side_effects=True, vmem_limit_bytes=40 << 20
        ),
        cost_estimate=pl.CostEstimate(
            flops=2 * STEPS * 2 * ROWS * 4096 * COLS, bytes_accessed=1 << 18, transcendentals=0
        ),
    )(density, pattern.T, keep_mask.T)


def solution(mesh):
    placed = (P("row", "col"), P("row", "col"), P("row", "col"))
    return jax.shard_map(
        per_device, mesh=mesh, in_specs=placed, out_specs=P("row", "col"), check_vma=False
    )
```
